128 devices in a mesh: dp: 8 (over y, core), seq: 16 (over z, x).
Axes of the slice: x: 4, y: 4, z: 4, core: 2. Of those that a mesh axis runs over, the one named last changes fastest.
Arguments:
- query: bfloat16 [16, 2048, 32, 128], P('dp', 'seq'), may hold values from -128 to 128
- keys: bfloat16 [16, 2048, 4, 128], P('dp', 'seq'), may hold values from -4.5 to 4.5
- values: bfloat16 [16, 2048, 4, 128], P('dp', 'seq'), may hold values from -6 to 6
- output: bfloat16 [16, 2048, 32, 128], P('dp', 'seq'), may hold values from -6 to 6
- out_grad: bfloat16 [16, 2048, 32, 128], P('dp', 'seq'), may hold values from -6 to 6
- lengths: int32 [16], P('dp'), may hold values from 341 to 2048, as said below
- margins: float32 [8], P('dp'), may hold values from -3 to 3
Outputs:
- query_grad: bfloat16 [16, 2048, 32, 128], P('dp', 'seq')
- key_grad: bfloat16 [16, 2048, 4, 128], P('dp', 'seq')
- value_grad: bfloat16 [16, 2048, 4, 128], P('dp', 'seq')
The draws below stay inside these ranges and needn't reach their ends.
Inputs may be any that keep to these rules, and one draw needn't show every extreme that they name: `lengths`: sequence 2p is pair p's chosen response and 2p + 1 its rejected one; some sequence has exactly 2048 tokens.
All inputs are finite; a program needn't handle non-finite values.
Results may differ from the reference program's by a relative error of at most 0.009.
Values may be sent and summed in bfloat16 or wider, within the bound.
No kernel may reach another device: no remote copies, remote signals or barrier semaphores. Data moves between devices by JAX's collectives and lax.ppermute only.
A program may use at most 128 MiB of HBM per device.

```python
import math
import jax
import jax.numpy as jnp
from jax import lax

HEADS = 32
KV_HEADS = 4
HEAD_DIM = 128
MAX_LEN = 2048
PAIRS_DEV = 1
PAIRS = 8
SEQS = 16
N_DP = 8


def key_base(key):
    base = jax.random.normal(jax.random.fold_in(key, 11), (SEQS, MAX_LEN, KV_HEADS, HEAD_DIM), jnp.float32)
    return jnp.clip(base, -4.5, 4.5)


def draw_keys(key, part):
    base = key_base(key)
    return base.astype(jnp.bfloat16)


def draw_query(key, part):
    fresh = jax.random.normal(jax.random.fold_in(key, 12), (SEQS, MAX_LEN, HEADS, HEAD_DIM), jnp.float32)
    fresh = jnp.clip(fresh, -4.5, 4.5)
    return fresh.astype(jnp.bfloat16)


def draw_lengths(key, part):
    index = jnp.arange(SEQS)
    group = index // (2 * PAIRS_DEV)
    third = MAX_LEN // 3
    upper = third + (MAX_LEN - third) * group // max(N_DP - 1, 1)
    lower = upper // 2
    raw = jax.random.randint(key, (SEQS,), 0, 1048576)
    length = lower + raw % (upper - lower + 1)
    length = jnp.where(index == (N_DP - 1) * 2 * PAIRS_DEV, MAX_LEN, length)
    length = jnp.where(index == 2 * PAIRS_DEV - 1, third // 2, length)
    return length.astype(jnp.int32)


def block_levels(rng, shape, shards, smallest, top_value):
    factor_of, own = 1.0, jax.random.fold_in(rng, 6)
    for dim, blocks in shards:
        steps = jnp.exp(jax.random.uniform(jax.random.fold_in(own, dim), (blocks,), jnp.float32, smallest / len(shards), top_value / len(shards)))
        factor_of = factor_of * jnp.repeat(steps, shape[dim] // blocks).reshape([-1 if axis == dim else 1 for axis in range(len(shape))])
    return factor_of


def bell_draw(own_key, dims, scale, limit, cuts=(), dtype=jnp.bfloat16):
    drawn = scale * jax.random.normal(own_key, dims, jnp.float32)
    if cuts:
        drawn = drawn * block_levels(own_key, dims, cuts, -0.22, 0.18)
    return jnp.clip(drawn, -limit, limit).astype(dtype)


def setup_inputs(seed: int = 0) -> dict:
    key_of = jax.random.split(jax.random.key(seed), 8)
    query = draw_query(jax.random.fold_in(key_of[7], 71), 0)
    keys = draw_keys(jax.random.fold_in(key_of[7], 71), 0)
    values = bell_draw(key_of[2], (SEQS, MAX_LEN, KV_HEADS, HEAD_DIM), 1.0, 6.0, ((0, 8), (1, 16)))
    output = bell_draw(key_of[3], (SEQS, MAX_LEN, HEADS, HEAD_DIM), 1.0, 6.0, ((0, 8), (1, 16)))
    out_grad = bell_draw(key_of[4], (SEQS, MAX_LEN, HEADS, HEAD_DIM), 1.0, 6.0, ((0, 8), (1, 16)))
    lengths = draw_lengths(jax.random.fold_in(key_of[7], 71), 0)
    margins = jnp.clip(jax.random.uniform(key_of[6], (PAIRS,), jnp.float32, -3.0, 3.0) * block_levels(key_of[6], (PAIRS,), ((0, 8),), -0.4, 0.0), -3.0, 3.0)
    return dict(query=query, keys=keys, values=values, output=output, out_grad=out_grad, lengths=lengths, margins=margins)


def sequence_grads(query, scaled, keys, values, delta):
    full_len, heads, head_dim = query.shape
    slots = keys.shape[1]
    repeat = heads // slots
    block = min(512, full_len)
    scale = 1.0 / math.sqrt(head_dim)
    q_four = query.reshape(full_len, slots, repeat, head_dim).astype(jnp.float32)
    g_four = scaled.reshape(full_len, slots, repeat, head_dim).astype(jnp.float32)
    d_three = delta.reshape(full_len, slots, repeat)
    keys_wide = keys.astype(jnp.float32)
    values_wide = values.astype(jnp.float32)
    key_pos = jnp.arange(full_len)
    key_acc = jnp.zeros((full_len, slots, head_dim), jnp.float32)
    value_acc = jnp.zeros((full_len, slots, head_dim), jnp.float32)
    pieces = []
    for index in range(full_len // block):
        start = index * block
        q_block = q_four[start:start + block]
        g_block = g_four[start:start + block]
        d_block = jnp.transpose(d_three[start:start + block], (1, 2, 0))[..., None]
        scores = jnp.einsum('isrd,jsd->srij', q_block, keys_wide) * scale
        query_pos = start + jnp.arange(block)
        causal = key_pos[None, :] <= query_pos[:, None]
        scores = jnp.where(causal, scores, -jnp.inf)
        top = lax.optimization_barrier(jnp.max(scores, axis=-1, keepdims=True))
        lse = top + jnp.log(lax.optimization_barrier(jnp.sum(jnp.exp(scores - top), axis=-1, keepdims=True)))
        prob = jnp.exp(scores - lse)
        prob_low = lax.optimization_barrier(prob.astype(jnp.bfloat16)).astype(jnp.float32)
        value_acc = value_acc + jnp.einsum('srij,isrd->jsd', prob_low, g_block)
        dprob = jnp.einsum('isrd,jsd->srij', g_block, values_wide)
        dscore = prob * (dprob - d_block)
        dscore_low = lax.optimization_barrier(dscore.astype(jnp.bfloat16)).astype(jnp.float32)
        query_part = jnp.einsum('srij,jsd->isrd', dscore_low, keys_wide) * scale
        pieces.append(query_part.reshape(block, heads, head_dim).astype(jnp.bfloat16))
        key_acc = key_acc + jnp.einsum('srij,isrd->jsd', dscore_low, q_block)
    query_grad = jnp.concatenate(pieces, axis=0)
    return (query_grad, (key_acc * scale).astype(jnp.bfloat16), value_acc.astype(jnp.bfloat16))

def reference(query, keys, values, output, out_grad, lengths, margins):
    seqs = query.shape[0]
    total = jnp.sum(lengths)
    mean_len = total.astype(jnp.float32) / seqs
    weight = jax.nn.sigmoid(-margins)
    signs = jnp.tile(jnp.array([-1.0, 1.0], jnp.float32), margins.shape[0])
    coef = jnp.repeat(weight, 2) * signs * 4.0 * mean_len / lengths.astype(jnp.float32)
    live = (jnp.arange(MAX_LEN).astype(jnp.int32)[None, :] < lengths[:, None]).astype(jnp.float32)
    factor = coef[:, None] * live
    scaled = (out_grad.astype(jnp.float32) * factor[:, :, None, None]).astype(jnp.bfloat16)
    delta = lax.optimization_barrier(jnp.sum(scaled.astype(jnp.float32) * output.astype(jnp.float32), axis=3))
    query_grad, key_grad, value_grad = lax.map(lambda items: sequence_grads(*items), (query, scaled, keys, values, delta))
    return (query_grad, key_grad, value_grad)
```

```python
import functools
import math

import jax
import jax.numpy as jnp
from jax import lax
from jax.experimental import pallas as pl
from jax.experimental.pallas import tpu as pltpu
from jax.sharding import PartitionSpec as P

f32, bf16 = jnp.float32, jnp.bfloat16
NT = (((1,), (1,)), ((), ()))
NN = (((1,), (0,)), ((), ()))

SIDE = 4
TOK = 128
GROUP = 8
DIM = 128
ROWS = TOK * GROUP
EXTRA = 16
FULL = TOK * SIDE * SIDE
CHUNK = 512
SCALE = 1.0 / math.sqrt(DIM)
EXP2 = SCALE * math.log2(math.e)
VMEM_BYTES = 56 * 1024 * 1024


def shift_pairs(kind, by):
    pairs = []
    for z in range(SIDE):
        for x in range(SIDE):
            to = ((z + by) % SIDE) * SIDE + x if kind == 0 else z * SIDE + (x + by) % SIDE
            pairs.append((z * SIDE + x, to))
    return pairs


def shift(value, kind, by):
    return lax.ppermute(value, "seq", shift_pairs(kind, by % SIDE))


def any_spec():
    return pl.BlockSpec(memory_space=pl.ANY)


def vmem_spec():
    return pl.BlockSpec(memory_space=pltpu.VMEM)


def smem_spec():
    return pl.BlockSpec(memory_space=pltpu.SMEM)


def params():
    return pltpu.CompilerParams(vmem_limit_bytes=VMEM_BYTES)


def pack_kv_kernel(place, kv_ref, *outs):
    for s in range(2):
        for d in range(SIDE):
            head = lax.rem(place[s] + d, SIDE)
            outs[s * SIDE + d][...] = kv_ref[s, head]


def pack_kernel(place, q_ref, g_ref, o_ref, *outs):
    for s in range(2):
        for d in range(SIDE):
            head = lax.rem(place[s] + d, SIDE)
            out = outs[s * SIDE + d]
            g = g_ref[s, :, head].reshape(ROWS, DIM)
            o = o_ref[s, :, head].reshape(ROWS, DIM)
            out[0:ROWS, :] = q_ref[s, :, head].reshape(ROWS, DIM)
            out[ROWS:2 * ROWS, :] = g
            prod = g.astype(f32) * o.astype(f32)
            high = prod.astype(bf16)
            low = (prod - high.astype(f32)).astype(bf16)
            ones = jnp.ones((8, DIM), bf16)
            delta = lax.dot_general(ones, high, NT, preferred_element_type=f32)
            delta += lax.dot_general(ones, low, NT, preferred_element_type=f32)
            rows = jnp.concatenate(
                [delta[0:1, a * DIM:(a + 1) * DIM] for a in range(ROWS // DIM)], axis=0
            )
            d_high = rows.astype(bf16)
            d_low = (rows - d_high.astype(f32)).astype(bf16)
            out[2 * ROWS:, :] = jnp.concatenate([d_high, d_low], axis=0)


def attention_kernel(meta, coef, *refs):
    packs, kvs = refs[0:SIDE], refs[SIDE:2 * SIDE]
    dqs, dkvs = refs[2 * SIDE:3 * SIDE], refs[3 * SIDE:4 * SIDE]
    pk, k_s, v_s, kt_s, p_s, m_s, dka, dva, gm_s, dqt_s, dq_s, sem_p, sem_kv, sem_o = refs[4 * SIDE:]
    length = meta[SIDE * SIDE]
    copies = []
    for d in range(SIDE):
        copies.append(pltpu.make_async_copy(packs[d], pk.at[d], sem_p.at[d]))
    for e in range(SIDE):
        for d in range(SIDE):
            at = pl.ds(pl.multiple_of(meta[e * SIDE + d] * TOK, TOK), TOK)
            slot = e * SIDE + d
            copies.append(
                pltpu.make_async_copy(kvs[e].at[d, pl.ds(0, TOK)], k_s.at[at], sem_kv.at[0, slot])
            )
            copies.append(
                pltpu.make_async_copy(kvs[e].at[d, pl.ds(TOK, TOK)], v_s.at[at], sem_kv.at[1, slot])
            )
    for copy in copies:
        copy.start()
    dka[...] = jnp.zeros_like(dka)
    dva[...] = jnp.zeros_like(dva)
    for copy in copies:
        copy.wait()
    kt_s[...] = k_s[...].T
    factor = coef[0]

    def one_block(d, _):
        block = meta[d]
        first = block * TOK

        @pl.when(first >= length)
        def _():
            dq_s[d] = jnp.zeros((ROWS, DIM), bf16)

        @pl.when(first < length)
        def _():
            token = lax.broadcasted_iota(jnp.int32, (ROWS, DIM), 0) // GROUP + first
            gm_s[...] = jnp.where(token < length, pk[d, ROWS:2 * ROWS, :], jnp.zeros((), bf16))
            lane_token = lax.broadcasted_iota(jnp.int32, (1, ROWS), 1) // GROUP + first
            tail = pk[d, 2 * ROWS:, :].astype(f32)
            tail = tail[0:8] + tail[8:16]
            delta = jnp.concatenate([tail[a:a + 1, :] for a in range(8)], axis=1)
            delta = jnp.where(lane_token < length, delta, 0.0)
            steps = (first + TOK + CHUNK - 1) // CHUNK

            def scores_step(c, carry, masked):
                top, total = carry
                k0 = pl.multiple_of(c * CHUNK, CHUNK)
                s = lax.dot_general(
                    k_s[pl.ds(k0, CHUNK), :], pk[d, 0:ROWS, :], NT, preferred_element_type=f32
                )
                if masked:
                    key = lax.broadcasted_iota(jnp.int32, (CHUNK, ROWS), 0) + k0
                    s = jnp.where(key <= lane_token, s, -jnp.inf)
                new = jnp.maximum(top, jnp.max(s, axis=0, keepdims=True))
                p = jnp.exp2((s - new) * EXP2)
                p_s[pl.ds(k0, CHUNK), :] = p
                m_s[c] = jnp.broadcast_to(new, (8, ROWS))
                total = total * jnp.exp2((top - new) * EXP2) + jnp.sum(p, axis=0, keepdims=True)
                return new, total

            carry = (jnp.full((1, ROWS), -1e30, f32), jnp.zeros((1, ROWS), f32))
            carry = lax.fori_loop(0, steps - 1, lambda c, x: scores_step(c, x, False), carry)
            top, total = scores_step(steps - 1, carry, True)
            inverse = 1.0 / total
            dqt_s[...] = jnp.zeros_like(dqt_s)

            def grads_step(c, _):
                k0 = pl.multiple_of(c * CHUNK, CHUNK)
                at = pl.ds(k0, CHUNK)
                g = gm_s[...]
                weight = jnp.exp2((m_s[c][0:1] - top) * EXP2) * inverse
                dp = lax.dot_general(v_s[at, :], g, NT, preferred_element_type=f32)
                prob = p_s[at, :] * weight
                ds = (prob * (dp - delta)).astype(bf16)
                dva[at, :] += lax.dot_general(prob.astype(bf16), g, NN, preferred_element_type=f32)
                dka[at, :] += lax.dot_general(ds, pk[d, 0:ROWS, :], NN, preferred_element_type=f32)
                dqt_s[...] += lax.dot_general(kt_s[:, at], ds, NN, preferred_element_type=f32)
                return 0

            lax.fori_loop(0, steps, grads_step, 0)
            dq_s[d] = (dqt_s[...].T * (factor * SCALE)).astype(bf16)

        return 0

    lax.fori_loop(0, SIDE, one_block, 0)
    outs = [pltpu.make_async_copy(dq_s.at[d], dqs[d], sem_o.at[d]) for d in range(SIDE)]
    for copy in outs:
        copy.start()
    for e in range(SIDE):
        for d in range(SIDE):
            at = pl.ds(pl.multiple_of(meta[e * SIDE + d] * TOK, TOK), TOK)
            dkvs[e][d, 0] = (dka[at, :] * (factor * SCALE)).astype(bf16)
            dkvs[e][d, 1] = (dva[at, :] * factor).astype(bf16)
    for copy in outs:
        copy.wait()


def attention(meta, coef, packs, kvs):
    flops = 2 * ROWS * FULL * DIM * 5 * SIDE // 2
    return pl.pallas_call(
        attention_kernel,
        in_specs=[smem_spec(), smem_spec()] + [any_spec()] * (2 * SIDE),
        out_specs=[any_spec()] * SIDE + [vmem_spec()] * SIDE,
        out_shape=[jax.ShapeDtypeStruct((ROWS, DIM), bf16)] * SIDE
        + [jax.ShapeDtypeStruct((SIDE, 2, TOK, DIM), bf16)] * SIDE,
        scratch_shapes=[
            pltpu.VMEM((SIDE, 2 * ROWS + EXTRA, DIM), bf16),
            pltpu.VMEM((FULL, DIM), bf16),
            pltpu.VMEM((FULL, DIM), bf16),
            pltpu.VMEM((DIM, FULL), bf16),
            pltpu.VMEM((FULL, ROWS), f32),
            pltpu.VMEM((FULL // CHUNK, 8, ROWS), f32),
            pltpu.VMEM((FULL, DIM), f32),
            pltpu.VMEM((FULL, DIM), f32),
            pltpu.VMEM((ROWS, DIM), bf16),
            pltpu.VMEM((DIM, ROWS), f32),
            pltpu.VMEM((SIDE, ROWS, DIM), bf16),
            pltpu.SemaphoreType.DMA((SIDE,)),
            pltpu.SemaphoreType.DMA((2, SIDE * SIDE)),
            pltpu.SemaphoreType.DMA((SIDE,)),
        ],
        compiler_params=params(),
        cost_estimate=pl.CostEstimate(flops=flops, bytes_accessed=8 << 20, transcendentals=ROWS * FULL * 2),
    )(meta, coef, *packs, *kvs)


def sum_kernel(a, b, c, d, *outs):
    for i in range(SIDE):
        total = a[i].astype(f32) + b[i].astype(f32) + (c[i].astype(f32) + d[i].astype(f32))
        outs[i][...] = total.astype(bf16)


def place_kernel(place, *refs):
    rows, out = refs[:-1], refs[-1]
    for s in range(2):
        for d in range(SIDE):
            head = lax.rem(place[s] + d, SIDE)
            out[s, :, head] = rows[s * SIDE + d][...].reshape(TOK, GROUP, DIM)


def place_kv_kernel(place, *refs):
    parts, out = refs[:-1], refs[-1]
    for s in range(2):
        for d in range(SIDE):
            out[s, lax.rem(place[s] + d, SIDE)] = parts[s * SIDE + d][...]


def body(query, keys, values, output, out_grad, lengths, margins):
    index = lax.axis_index("seq")
    z, x = index // SIDE, index % SIDE
    place = jnp.stack([z, x]).astype(jnp.int32)
    cross = [x, z]
    total = lax.psum(jnp.sum(lengths), "dp")
    mean_len = total.astype(f32) / (2 * lax.axis_size("dp"))
    weight = jax.nn.sigmoid(-margins)
    signs = jnp.array([-1.0, 1.0], f32)
    coef = jnp.repeat(weight, 2) * signs * 4.0 * mean_len / lengths.astype(f32)

    kv = jnp.stack([keys, values], axis=0)
    kv = jnp.transpose(kv, (1, 3, 0, 2, 4)).reshape(2, SIDE, 2 * TOK, DIM)
    kv_parts = pl.pallas_call(
        pack_kv_kernel,
        in_specs=[smem_spec(), vmem_spec()],
        out_specs=[vmem_spec()] * (2 * SIDE),
        out_shape=[jax.ShapeDtypeStruct((2 * TOK, DIM), bf16)] * (2 * SIDE),
        compiler_params=params(),
    )(place, kv)
    five = (2, TOK, SIDE, GROUP, DIM)
    packs = pl.pallas_call(
        pack_kernel,
        in_specs=[smem_spec()] + [vmem_spec()] * 3,
        out_specs=[vmem_spec()] * (2 * SIDE),
        out_shape=[jax.ShapeDtypeStruct((2 * ROWS + EXTRA, DIM), bf16)] * (2 * SIDE),
        compiler_params=params(),
    )(place, query.reshape(five), out_grad.reshape(five), output.reshape(five))

    gathered, moved = [], []
    for s in range(2):
        kv_in = [kv_parts[s * SIDE]] + [shift(kv_parts[s * SIDE + d], s, d) for d in range(1, SIDE)]
        mine = jnp.stack(kv_in, axis=0)
        gathered.append([mine] + [shift(mine, 1 - s, e) for e in range(1, SIDE)])
        moved.append([packs[s * SIDE]] + [shift(packs[s * SIDE + d], s, d) for d in range(1, SIDE)])

    dq_rows, kv_grads = [], []
    for s in range(2):
        order = []
        for e in range(SIDE):
            for d in range(SIDE):
                along, across = (place[s] - d) % SIDE, (cross[s] - e) % SIDE
                order.append(along * SIDE + across if s == 0 else across * SIDE + along)
        meta = jnp.stack(order + [lengths[s]]).astype(jnp.int32)
        res = attention(meta, coef[s].reshape(1), moved[s], gathered[s])
        dqs, dkvs = res[:SIDE], res[SIDE:]
        dq_rows += [dqs[0]] + [shift(dqs[d], s, -d) for d in range(1, SIDE)]
        sums = [dkvs[0]] + [shift(dkvs[e], 1 - s, -e) for e in range(1, SIDE)]
        parts = pl.pallas_call(
            sum_kernel,
            in_specs=[vmem_spec()] * SIDE,
            out_specs=[vmem_spec()] * SIDE,
            out_shape=[jax.ShapeDtypeStruct((2, TOK, DIM), bf16)] * SIDE,
            compiler_params=params(),
        )(*sums)
        kv_grads += [parts[0]] + [shift(parts[d], s, -d) for d in range(1, SIDE)]

    query_grad = pl.pallas_call(
        place_kernel,
        in_specs=[smem_spec()] + [vmem_spec()] * (2 * SIDE),
        out_specs=vmem_spec(),
        out_shape=jax.ShapeDtypeStruct(five, bf16),
        compiler_params=params(),
    )(place, *dq_rows).reshape(query.shape)
    kv_grad = pl.pallas_call(
        place_kv_kernel,
        in_specs=[smem_spec()] + [vmem_spec()] * (2 * SIDE),
        out_specs=vmem_spec(),
        out_shape=jax.ShapeDtypeStruct((2, SIDE, 2, TOK, DIM), bf16),
        compiler_params=params(),
    )(place, *kv_grads)
    kv_grad = jnp.transpose(kv_grad, (2, 0, 3, 1, 4))
    return (query_grad, kv_grad[0], kv_grad[1])


def solution(mesh):
    spec = P("dp", "seq", None, None)
    return jax.shard_map(
        body,
        mesh=mesh,
        in_specs=(spec,) * 5 + (P("dp"), P("dp")),
        out_specs=(spec,) * 3,
        check_vma=False,
    )
```

```python
import functools
import math

import jax
import jax.numpy as jnp
from jax import lax
from jax.experimental import pallas as pl
from jax.experimental.pallas import tpu as pltpu
from jax.sharding import PartitionSpec as P

f32, bf16 = jnp.float32, jnp.bfloat16
NT = (((1,), (1,)), ((), ()))
NN = (((1,), (0,)), ((), ()))

SIDE = 4
TOK = 128
GROUP = 8
DIM = 128
ROWS = TOK * GROUP
EXTRA = 16
FULL = TOK * SIDE * SIDE
CHUNK = 512
SCALE = 1.0 / math.sqrt(DIM)
EXP2 = SCALE * math.log2(math.e)
VMEM_BYTES = 56 * 1024 * 1024


def shift_pairs(kind, by):
    pairs = []
    for z in range(SIDE):
        for x in range(SIDE):
            to = ((z + by) % SIDE) * SIDE + x if kind == 0 else z * SIDE + (x + by) % SIDE
            pairs.append((z * SIDE + x, to))
    return pairs


def shift(value, kind, by):
    return lax.ppermute(value, "seq", shift_pairs(kind, by % SIDE))


def any_spec():
    return pl.BlockSpec(memory_space=pl.ANY)


def vmem_spec():
    return pl.BlockSpec(memory_space=pltpu.VMEM)


def smem_spec():
    return pl.BlockSpec(memory_space=pltpu.SMEM)


def params():
    return pltpu.CompilerParams(vmem_limit_bytes=VMEM_BYTES)


def pack_kernel(place, q_ref, g_ref, o_ref, *outs):
    for d in range(SIDE):
        head = lax.rem(place[0] + d, SIDE)
        out = outs[d]
        g = g_ref[:, head].reshape(ROWS, DIM)
        o = o_ref[:, head].reshape(ROWS, DIM)
        out[0:ROWS, :] = q_ref[:, head].reshape(ROWS, DIM)
        out[ROWS:2 * ROWS, :] = g
        prod = g.astype(f32) * o.astype(f32)
        high = prod.astype(bf16)
        low = (prod - high.astype(f32)).astype(bf16)
        ones = jnp.ones((8, DIM), bf16)
        delta = lax.dot_general(ones, high, NT, preferred_element_type=f32)
        delta += lax.dot_general(ones, low, NT, preferred_element_type=f32)
        rows = jnp.concatenate(
            [delta[0:1, a * DIM:(a + 1) * DIM] for a in range(ROWS // DIM)], axis=0
        )
        d_high = rows.astype(bf16)
        d_low = (rows - d_high.astype(f32)).astype(bf16)
        out[2 * ROWS:, :] = jnp.concatenate([d_high, d_low], axis=0)


def pack(place, s, query, out_grad, output):
    block = (None, TOK, SIDE, GROUP, DIM)
    spec = pl.BlockSpec(block, lambda i: (s, 0, 0, 0, 0))
    return pl.pallas_call(
        pack_kernel,
        grid=(1,),
        in_specs=[smem_spec()] + [spec] * 3,
        out_specs=[vmem_spec()] * SIDE,
        out_shape=[jax.ShapeDtypeStruct((2 * ROWS + EXTRA, DIM), bf16)] * SIDE,
        compiler_params=params(),
    )(place, query, out_grad, output)


def token_block(z, x, d, e):
    return lax.rem(z - d + SIDE, SIDE) * SIDE + lax.rem(x - e + SIDE, SIDE)


def attention_kernel(seq, shifts, first_call, last_call, *refs):
    count = len(shifts)
    refs = list(refs)
    meta, coef = refs[:2]
    packs = refs[2:2 + count]
    kvs = refs[2 + count:2 + count + SIDE]
    refs = refs[2 + count + SIDE:]
    if not first_call:
        acc_in, refs = refs[:2], refs[2:]
    dqs, refs = refs[:count], refs[count:]
    if last_call:
        dkv, refs = refs[0], refs[1:]
        dka, dva = refs[:2]
        refs = refs[2:]
    else:
        dka, dva = refs[:2]
        refs = refs[2:]
    pk, k_s, v_s, kt_s, p_s, m_s, gm_s, dqt_s, dq_s, sem_p, sem_kv, sem_o = refs
    z, x, length = meta[0], meta[1], meta[2 + seq]
    copies = []
    for e in range(SIDE):
        for d in range(SIDE):
            at, slot = token_block(z, x, d, e), e * SIDE + d
            copies.append(pltpu.make_async_copy(kvs[e].at[d, 0], k_s.at[at], sem_kv.at[0, slot]))
            copies.append(pltpu.make_async_copy(kvs[e].at[d, 1], v_s.at[at], sem_kv.at[1, slot]))
    for d in range(count):
        copies.append(pltpu.make_async_copy(packs[d], pk.at[d], sem_p.at[d]))
    for copy in copies:
        copy.start()
    if first_call:
        dka[...] = jnp.zeros_like(dka)
        dva[...] = jnp.zeros_like(dva)
    else:
        dka[...] = acc_in[0][...]
        dva[...] = acc_in[1][...]
    for copy in copies:
        copy.wait()
    kt_s[...] = k_s[...].reshape(FULL, DIM).T
    factor = coef[seq]
    along = [token_block(z, x, d, 0) for d in shifts]

    def one_block(d, _):
        block = along[0]
        for n in range(1, count):
            block = jnp.where(d == n, along[n], block)
        first = block * TOK

        @pl.when(first >= length)
        def _():
            dq_s[d] = jnp.zeros((ROWS, DIM), bf16)

        @pl.when(first < length)
        def _():
            token = lax.broadcasted_iota(jnp.int32, (ROWS, DIM), 0) // GROUP + first
            gm_s[...] = jnp.where(token < length, pk[d, ROWS:2 * ROWS, :], jnp.zeros((), bf16))
            lane_token = lax.broadcasted_iota(jnp.int32, (1, ROWS), 1) // GROUP + first
            tail = pk[d, 2 * ROWS:, :].astype(f32)
            tail = tail[0:8] + tail[8:16]
            delta = jnp.concatenate([tail[a:a + 1, :] for a in range(8)], axis=1)
            delta = jnp.where(lane_token < length, delta, 0.0)
            steps = (first + TOK + CHUNK - 1) // CHUNK

            def blocks(c):
                return pl.ds(c * (CHUNK // TOK), CHUNK // TOK)

            def scores_step(c, carry, masked):
                top, total = carry
                k0 = pl.multiple_of(c * CHUNK, CHUNK)
                s = lax.dot_general(
                    k_s[blocks(c)].reshape(CHUNK, DIM),
                    pk[d, 0:ROWS, :],
                    NT,
                    preferred_element_type=f32,
                )
                if masked:
                    key = lax.broadcasted_iota(jnp.int32, (CHUNK, ROWS), 0) + k0
                    s = jnp.where(key <= lane_token, s, -jnp.inf)
                new = jnp.maximum(top, jnp.max(s, axis=0, keepdims=True))
                p = jnp.exp2((s - new) * EXP2)
                p_s[pl.ds(k0, CHUNK), :] = p
                m_s[c] = jnp.broadcast_to(new, (8, ROWS))
                total = total * jnp.exp2((top - new) * EXP2) + jnp.sum(p, axis=0, keepdims=True)
                return new, total

            carry = (jnp.full((1, ROWS), -1e30, f32), jnp.zeros((1, ROWS), f32))
            carry = lax.fori_loop(0, steps - 1, lambda c, x: scores_step(c, x, False), carry)
            top, total = scores_step(steps - 1, carry, True)
            inverse = 1.0 / total
            dqt_s[...] = jnp.zeros_like(dqt_s)

            def grads_step(c, _):
                k0 = pl.multiple_of(c * CHUNK, CHUNK)
                at = pl.ds(k0, CHUNK)
                g = gm_s[...]
                weight = jnp.exp2((m_s[c][0:1] - top) * EXP2) * inverse
                dp = lax.dot_general(
                    v_s[blocks(c)].reshape(CHUNK, DIM), g, NT, preferred_element_type=f32
                )
                prob = p_s[at, :] * weight
                ds = (prob * (dp - delta)).astype(bf16)
                dva[at, :] += lax.dot_general(prob.astype(bf16), g, NN, preferred_element_type=f32)
                dka[at, :] += lax.dot_general(ds, pk[d, 0:ROWS, :], NN, preferred_element_type=f32)
                dqt_s[...] += lax.dot_general(kt_s[:, at], ds, NN, preferred_element_type=f32)
                return 0

            lax.fori_loop(0, steps, grads_step, 0)
            dq_s[d] = (dqt_s[...].T * (factor * SCALE)).astype(bf16)

        return 0

    lax.fori_loop(0, count, one_block, 0)
    outs = [pltpu.make_async_copy(dq_s.at[d], dqs[d], sem_o.at[d]) for d in range(count)]
    for copy in outs:
        copy.start()
    if last_call:
        for b in range(FULL // TOK):
            at = pl.ds(b * TOK, TOK)
            dkv[b, 0] = (dka[at, :] * (factor * SCALE)).astype(bf16)
            dkv[b, 1] = (dva[at, :] * factor).astype(bf16)
    for copy in outs:
        copy.wait()


def attention(meta, coef, seq, shifts, packs, kvs, acc_in=None, last_call=True):
    count = len(packs)
    first_call = acc_in is None
    acc = jax.ShapeDtypeStruct((FULL, DIM), f32)
    acc_scratch = [pltpu.VMEM((FULL, DIM), f32)] * 2
    out_shape = [jax.ShapeDtypeStruct((ROWS, DIM), bf16)] * count
    out_specs = [any_spec()] * count
    if last_call:
        out_shape += [jax.ShapeDtypeStruct((FULL // TOK, 2, TOK, DIM), bf16)]
        out_specs += [vmem_spec()]
    else:
        out_shape += [acc, acc]
        out_specs += [vmem_spec()] * 2
    return pl.pallas_call(
        functools.partial(attention_kernel, seq, shifts, first_call, last_call),
        in_specs=[smem_spec(), smem_spec()]
        + [any_spec()] * (count + SIDE)
        + [vmem_spec()] * (0 if first_call else 2),
        out_specs=out_specs,
        out_shape=out_shape,
        scratch_shapes=(acc_scratch if last_call else [])
        + [
            pltpu.VMEM((count, 2 * ROWS + EXTRA, DIM), bf16),
            pltpu.VMEM((FULL // TOK, TOK, DIM), bf16),
            pltpu.VMEM((FULL // TOK, TOK, DIM), bf16),
            pltpu.VMEM((DIM, FULL), bf16),
            pltpu.VMEM((FULL, ROWS), f32),
            pltpu.VMEM((FULL // CHUNK, 8, ROWS), f32),
            pltpu.VMEM((ROWS, DIM), bf16),
            pltpu.VMEM((DIM, ROWS), f32),
            pltpu.VMEM((count, ROWS, DIM), bf16),
            pltpu.SemaphoreType.DMA((count,)),
            pltpu.SemaphoreType.DMA((2, SIDE * SIDE)),
            pltpu.SemaphoreType.DMA((count,)),
        ],
        compiler_params=params(),
        cost_estimate=pl.CostEstimate(
            flops=2 * ROWS * FULL * DIM * 5 * count,
            bytes_accessed=8 << 20,
            transcendentals=ROWS * FULL * count,
        ),
    )(meta, coef, *packs, *kvs, *(() if first_call else acc_in))


def place_kernel(place, mean_len, *refs):
    rows, out = refs[:-1], refs[-1]
    for s in range(2):
        for d in range(SIDE):
            head = lax.rem(place[0] + d, SIDE)
            grad = rows[s * SIDE + d][...].astype(f32) * mean_len[0]
            out[s, :, head] = grad.astype(bf16).reshape(TOK, GROUP, DIM)


ROUNDS = (((3, 0, 1, 2),), ((2, 1, 3, 0),))


def after(value, other):
    return lax.optimization_barrier((value, other))[0]


def pack_kv_kernel(place, kv_ref, *outs):
    for d in range(SIDE):
        outs[d][...] = kv_ref[lax.rem(place[0] + d, SIDE)]


def body(query, keys, values, output, out_grad, lengths, margins):
    index = lax.axis_index("seq")
    z, x = index // SIDE, index % SIDE
    place = jnp.concatenate([jnp.stack([z, x]).astype(jnp.int32), lengths])
    weight = jax.nn.sigmoid(-margins)
    signs = jnp.array([-1.0, 1.0], f32)
    coef = jnp.repeat(weight, 2) * signs * 4.0 / lengths.astype(f32)

    kv = jnp.stack([keys, values], axis=1)
    kv = jnp.transpose(kv, (3, 0, 1, 2, 4))
    kv_parts = pl.pallas_call(
        pack_kv_kernel,
        in_specs=[smem_spec(), vmem_spec()],
        out_specs=[vmem_spec()] * SIDE,
        out_shape=[jax.ShapeDtypeStruct((2, 2, TOK, DIM), bf16)] * SIDE,
        compiler_params=params(),
    )(place, kv)
    kv_in = [kv_parts[0]] + [shift(kv_parts[d], 0, d) for d in range(1, SIDE)]
    five = (2, TOK, SIDE, GROUP, DIM)
    query, out_grad, output = (a.reshape(five) for a in (query, out_grad, output))
    query = after(query, kv_parts)
    packs = [pack(place, s, query, out_grad, output) for s in range(2)]
    kv_in = after(kv_in, packs[0])
    gathered = []
    for s in range(2):
        mine = jnp.stack([part[s] for part in kv_in], axis=0)
        gathered.append([mine] + [shift(mine, 1, e) for e in (1, 2, 3)])

    moved = []
    for s in range(2):
        mine = packs[s] if s == 0 else after(packs[s], gathered[0])
        moved.append([mine[0]] + [shift(mine[d], 0, d) for d in range(1, SIDE)])

    dq_rows, kv_grads, prev = [], [], None
    for s in range(2):
        meta = place if s == 0 else after(place, prev)
        acc, dqs = None, {}
        for n, shifts in enumerate(ROUNDS[s]):
            last = n == len(ROUNDS[s]) - 1
            packs_now = [moved[s][d] for d in shifts]
            res = attention(meta, coef, s, shifts, packs_now, gathered[s], acc, last)
            if last:
                prev = after(res[len(shifts)], list(dqs.values()) + dq_rows)
            else:
                acc = res[len(shifts):]
            for d, dq in zip(shifts, res):
                dqs[d] = dq if d == 0 else shift(dq, 0, -d)
        dq_rows += [dqs[d] for d in range(SIDE)]
        parts = lax.all_to_all(prev, "seq", 0, 0, tiled=True)
        parts = parts.reshape(SIDE, SIDE, 2, TOK, DIM).astype(f32)
        kv_grads.append(jnp.sum(parts, axis=1))

    total = lax.psum(jnp.sum(after(lengths, prev)), "dp")
    mean_len = total.astype(f32) / (2 * lax.axis_size("dp"))
    query_grad = pl.pallas_call(
        place_kernel,
        in_specs=[smem_spec()] * 2 + [vmem_spec()] * (2 * SIDE),
        out_specs=vmem_spec(),
        out_shape=jax.ShapeDtypeStruct(five, bf16),
        compiler_params=params(),
    )(place, mean_len.reshape(1), *dq_rows).reshape(2, TOK, SIDE * GROUP, DIM)
    kv_grad = jnp.transpose(jnp.stack(kv_grads, axis=0) * mean_len, (2, 0, 3, 1, 4)).astype(bf16)
    return (query_grad, kv_grad[0], kv_grad[1])


def solution(mesh):
    spec = P("dp", "seq", None, None)
    return jax.shard_map(
        body,
        mesh=mesh,
        in_specs=(spec,) * 5 + (P("dp"), P("dp")),
        out_specs=(spec,) * 3,
        check_vma=False,
    )
```

```python
import functools
import math

import jax
import jax.numpy as jnp
from jax import lax
from jax.experimental import pallas as pl
from jax.experimental.pallas import tpu as pltpu
from jax.sharding import PartitionSpec as P

f32, bf16 = jnp.float32, jnp.bfloat16
NT = (((1,), (1,)), ((), ()))
NN = (((1,), (0,)), ((), ()))

SIDE = 4
TOK = 128
GROUP = 8
DIM = 128
ROWS = TOK * GROUP
EXTRA = 16
FULL = TOK * SIDE * SIDE
CHUNK = 512
SCALE = 1.0 / math.sqrt(DIM)
EXP2 = SCALE * math.log2(math.e)
VMEM_BYTES = 56 * 1024 * 1024


def shift_pairs(kind, by):
    pairs = []
    for z in range(SIDE):
        for x in range(SIDE):
            to = ((z + by) % SIDE) * SIDE + x if kind == 0 else z * SIDE + (x + by) % SIDE
            pairs.append((z * SIDE + x, to))
    return pairs


def shift(value, kind, by):
    return lax.ppermute(value, "seq", shift_pairs(kind, by % SIDE))


def any_spec():
    return pl.BlockSpec(memory_space=pl.ANY)


def vmem_spec():
    return pl.BlockSpec(memory_space=pltpu.VMEM)


def smem_spec():
    return pl.BlockSpec(memory_space=pltpu.SMEM)


def params():
    return pltpu.CompilerParams(vmem_limit_bytes=VMEM_BYTES)


def pack_kernel(place, q_ref, g_ref, o_ref, *outs):
    for d in range(SIDE):
        head = lax.rem(place[0] + d, SIDE)
        out = outs[d]
        g = g_ref[:, head].reshape(ROWS, DIM)
        o = o_ref[:, head].reshape(ROWS, DIM)
        out[0:ROWS, :] = q_ref[:, head].reshape(ROWS, DIM)
        out[ROWS:2 * ROWS, :] = g
        prod = g.astype(f32) * o.astype(f32)
        high = prod.astype(bf16)
        low = (prod - high.astype(f32)).astype(bf16)
        ones = jnp.ones((8, DIM), bf16)
        delta = lax.dot_general(ones, high, NT, preferred_element_type=f32)
        delta += lax.dot_general(ones, low, NT, preferred_element_type=f32)
        rows = jnp.concatenate(
            [delta[0:1, a * DIM:(a + 1) * DIM] for a in range(ROWS // DIM)], axis=0
        )
        d_high = rows.astype(bf16)
        d_low = (rows - d_high.astype(f32)).astype(bf16)
        out[2 * ROWS:, :] = jnp.concatenate([d_high, d_low], axis=0)


def pack(place, s, query, out_grad, output):
    block = (None, TOK, SIDE, GROUP, DIM)
    spec = pl.BlockSpec(block, lambda i: (s, 0, 0, 0, 0))
    return pl.pallas_call(
        pack_kernel,
        grid=(1,),
        in_specs=[smem_spec()] + [spec] * 3,
        out_specs=[vmem_spec()] * SIDE,
        out_shape=[jax.ShapeDtypeStruct((2 * ROWS + EXTRA, DIM), bf16)] * SIDE,
        compiler_params=params(),
    )(place, query, out_grad, output)


def token_block(z, x, d, e):
    return lax.rem(z - d + SIDE, SIDE) * SIDE + lax.rem(x - e + SIDE, SIDE)


def attention_kernel(seq, shifts, first_call, last_call, *refs):
    count = len(shifts)
    refs = list(refs)
    meta, coef = refs[:2]
    packs = refs[2:2 + count]
    kvs = refs[2 + count:2 + count + SIDE]
    refs = refs[2 + count + SIDE:]
    if not first_call:
        acc_in, refs = refs[:2], refs[2:]
    dqs, refs = refs[:count], refs[count:]
    if last_call:
        dkv, refs = refs[0], refs[1:]
        dka, dva = refs[:2]
        refs = refs[2:]
    else:
        dka, dva = refs[:2]
        refs = refs[2:]
    pk, k_s, v_s, kt_s, p_s, m_s, gm_s, dqt_s, stat, dq_s, sem_p, sem_kv, sem_o = refs
    z, x, length = meta[0], meta[1], meta[2 + seq]
    copies = []
    for e in range(SIDE):
        for d in range(SIDE):
            at, slot = token_block(z, x, d, e), e * SIDE + d
            copies.append(pltpu.make_async_copy(kvs[e].at[d, 0], k_s.at[at], sem_kv.at[0, slot]))
            copies.append(pltpu.make_async_copy(kvs[e].at[d, 1], v_s.at[at], sem_kv.at[1, slot]))
    for d in range(count):
        copies.append(pltpu.make_async_copy(packs[d], pk.at[d], sem_p.at[d]))
    for copy in copies:
        copy.start()
    if first_call:
        dka[...] = jnp.zeros_like(dka)
        dva[...] = jnp.zeros_like(dva)
    else:
        dka[...] = acc_in[0][...]
        dva[...] = acc_in[1][...]
    for copy in copies[:2 * SIDE * SIDE]:
        copy.wait()
    kt_s[...] = k_s[...].reshape(FULL, DIM).T
    factor = coef[seq]
    along = [token_block(z, x, d, 0) for d in shifts]

    def one_block(d, _):
        block = along[0]
        for n in range(1, count):
            block = jnp.where(d == n, along[n], block)
        first = block * TOK
        pltpu.make_async_copy(pk.at[d], pk.at[d], sem_p.at[d]).wait()

        @pl.when(first >= length)
        def _():
            dq_s[d] = jnp.zeros((ROWS, DIM), bf16)

        @pl.when(first < length)
        def _():
            token = lax.broadcasted_iota(jnp.int32, (ROWS, DIM), 0) // GROUP + first
            gm_s[...] = jnp.where(token < length, pk[d, ROWS:2 * ROWS, :], jnp.zeros((), bf16))
            lane_token = lax.broadcasted_iota(jnp.int32, (1, ROWS), 1) // GROUP + first
            tail = pk[d, 2 * ROWS:, :].astype(f32)
            tail = tail[0:8] + tail[8:16]
            delta = jnp.concatenate([tail[a:a + 1, :] for a in range(8)], axis=1)
            delta = jnp.where(lane_token < length, delta, 0.0)
            steps = (first + TOK + CHUNK - 1) // CHUNK

            per = CHUNK // TOK
            rest = lax.rem(block, per) + 1

            def scores_step(c, width, carry, masked):
                top, total = carry
                k0 = pl.multiple_of(c * CHUNK, CHUNK)
                s = lax.dot_general(
                    k_s[pl.ds(c * per, width)].reshape(width * TOK, DIM),
                    pk[d, 0:ROWS, :],
                    NT,
                    preferred_element_type=f32,
                )
                if masked:
                    key = lax.broadcasted_iota(jnp.int32, (width * TOK, ROWS), 0) + k0
                    s = jnp.where(key <= lane_token, s, -jnp.inf)
                new = jnp.maximum(top, jnp.max(s, axis=0, keepdims=True))
                p = jnp.exp2((s - new) * EXP2)
                p_s[pl.ds(k0, width * TOK), :] = p
                m_s[c] = jnp.broadcast_to(new, (8, ROWS))
                total = total * jnp.exp2((top - new) * EXP2) + jnp.sum(p, axis=0, keepdims=True)
                return new, total

            carry = (jnp.full((1, ROWS), -1e30, f32), jnp.zeros((1, ROWS), f32))
            carry = lax.fori_loop(
                0, steps - 1, lambda c, held: scores_step(c, per, held, False), carry
            )
            for width in range(1, per + 1):

                @pl.when(rest == width)
                def _():
                    row_top, row_total = scores_step(steps - 1, width, carry, True)
                    stat[0:1, :] = row_top
                    stat[8:9, :] = row_total

            top, total = stat[0:1, :], stat[8:9, :]
            inverse = 1.0 / total
            dqt_s[...] = jnp.zeros_like(dqt_s)

            def grads_step(c, width):
                k0 = pl.multiple_of(c * CHUNK, CHUNK)
                at = pl.ds(k0, width * TOK)
                g = gm_s[...]
                weight = jnp.exp2((m_s[c][0:1] - top) * EXP2) * inverse
                dp = lax.dot_general(
                    v_s[pl.ds(c * per, width)].reshape(width * TOK, DIM), g, NT, preferred_element_type=f32
                )
                prob = p_s[at, :] * weight
                ds = (prob * (dp - delta)).astype(bf16)
                dva[at, :] += lax.dot_general(prob.astype(bf16), g, NN, preferred_element_type=f32)
                dka[at, :] += lax.dot_general(ds, pk[d, 0:ROWS, :], NN, preferred_element_type=f32)
                dqt_s[...] += lax.dot_general(kt_s[:, at], ds, NN, preferred_element_type=f32)

            def full_step(c, _):
                grads_step(c, per)
                return 0

            lax.fori_loop(0, steps - 1, full_step, 0)
            for width in range(1, per + 1):

                @pl.when(rest == width)
                def _():
                    grads_step(steps - 1, width)

            dq_s[d] = (dqt_s[...].T * (factor * SCALE)).astype(bf16)

        return 0

    lax.fori_loop(0, count, one_block, 0)
    outs = [pltpu.make_async_copy(dq_s.at[d], dqs[d], sem_o.at[d]) for d in range(count)]
    for copy in outs:
        copy.start()
    if last_call:
        for b in range(FULL // TOK):
            at = pl.ds(b * TOK, TOK)
            dkv[b, 0] = (dka[at, :] * (factor * SCALE)).astype(bf16)
            dkv[b, 1] = (dva[at, :] * factor).astype(bf16)
    for copy in outs:
        copy.wait()


def attention(meta, coef, seq, shifts, packs, kvs, acc_in=None, last_call=True):
    count = len(packs)
    first_call = acc_in is None
    acc = jax.ShapeDtypeStruct((FULL, DIM), f32)
    acc_scratch = [pltpu.VMEM((FULL, DIM), f32)] * 2
    out_shape = [jax.ShapeDtypeStruct((ROWS, DIM), bf16)] * count
    out_specs = [any_spec()] * count
    if last_call:
        out_shape += [jax.ShapeDtypeStruct((FULL // TOK, 2, TOK, DIM), bf16)]
        out_specs += [vmem_spec()]
    else:
        out_shape += [acc, acc]
        out_specs += [vmem_spec()] * 2
    return pl.pallas_call(
        functools.partial(attention_kernel, seq, shifts, first_call, last_call),
        in_specs=[smem_spec(), smem_spec()]
        + [any_spec()] * (count + SIDE)
        + [vmem_spec()] * (0 if first_call else 2),
        out_specs=out_specs,
        out_shape=out_shape,
        scratch_shapes=(acc_scratch if last_call else [])
        + [
            pltpu.VMEM((count, 2 * ROWS + EXTRA, DIM), bf16),
            pltpu.VMEM((FULL // TOK, TOK, DIM), bf16),
            pltpu.VMEM((FULL // TOK, TOK, DIM), bf16),
            pltpu.VMEM((DIM, FULL), bf16),
            pltpu.VMEM((FULL, ROWS), f32),
            pltpu.VMEM((FULL // CHUNK, 8, ROWS), f32),
            pltpu.VMEM((ROWS, DIM), bf16),
            pltpu.VMEM((DIM, ROWS), f32),
            pltpu.VMEM((16, ROWS), f32),
            pltpu.VMEM((count, ROWS, DIM), bf16),
            pltpu.SemaphoreType.DMA((count,)),
            pltpu.SemaphoreType.DMA((2, SIDE * SIDE)),
            pltpu.SemaphoreType.DMA((count,)),
        ],
        compiler_params=params(),
        cost_estimate=pl.CostEstimate(
            flops=2 * ROWS * FULL * DIM * 5 * count,
            bytes_accessed=8 << 20,
            transcendentals=ROWS * FULL * count,
        ),
    )(meta, coef, *packs, *kvs, *(() if first_call else acc_in))


def place_kernel(place, mean_len, *refs):
    rows, out = refs[:-1], refs[-1]
    for s in range(2):
        for d in range(SIDE):
            head = lax.rem(place[0] + d, SIDE)
            grad = rows[s * SIDE + d][...].astype(f32) * mean_len[0]
            out[s, :, head] = grad.astype(bf16).reshape(TOK, GROUP, DIM)


ROUNDS = (((3, 0, 1, 2),), ((2, 1, 3, 0),))


def after(value, other):
    return lax.optimization_barrier((value, other))[0]


def pack_kv_kernel(place, kv_ref, *outs):
    for d in range(SIDE):
        outs[d][...] = kv_ref[lax.rem(place[0] + d, SIDE)]


def body(query, keys, values, output, out_grad, lengths, margins):
    index = lax.axis_index("seq")
    z, x = index // SIDE, index % SIDE
    place = jnp.concatenate([jnp.stack([z, x]).astype(jnp.int32), lengths])
    weight = jax.nn.sigmoid(-margins)
    signs = jnp.array([-1.0, 1.0], f32)
    coef = jnp.repeat(weight, 2) * signs * 4.0 / lengths.astype(f32)

    kv = jnp.stack([keys, values], axis=1)
    kv = jnp.transpose(kv, (3, 0, 1, 2, 4))
    kv_parts = pl.pallas_call(
        pack_kv_kernel,
        in_specs=[smem_spec(), vmem_spec()],
        out_specs=[vmem_spec()] * SIDE,
        out_shape=[jax.ShapeDtypeStruct((2, 2, TOK, DIM), bf16)] * SIDE,
        compiler_params=params(),
    )(place, kv)
    kv_in = [kv_parts[0]] + [shift(kv_parts[d], 0, d) for d in range(1, SIDE)]
    five = (2, TOK, SIDE, GROUP, DIM)
    query, out_grad, output = (a.reshape(five) for a in (query, out_grad, output))
    query = after(query, kv_parts)
    packs = [pack(place, s, query, out_grad, output) for s in range(2)]
    kv_in = after(kv_in, packs[0])
    gathered = []
    for s in range(2):
        mine = jnp.stack([part[s] for part in kv_in], axis=0)
        gathered.append([mine] + [shift(mine, 1, e) for e in (1, 2, 3)])

    moved = []
    for s in range(2):
        mine = packs[s] if s == 0 else after(packs[s], gathered[0])
        moved.append([mine[0]] + [shift(mine[d], 0, d) for d in range(1, SIDE)])

    dq_rows, kv_grads, prev = [], [], None
    for s in range(2):
        meta = place if s == 0 else after(place, prev)
        acc, dqs = None, {}
        for n, shifts in enumerate(ROUNDS[s]):
            last = n == len(ROUNDS[s]) - 1
            packs_now = [moved[s][d] for d in shifts]
            res = attention(meta, coef, s, shifts, packs_now, gathered[s], acc, last)
            if last:
                prev = after(res[len(shifts)], list(dqs.values()) + dq_rows)
            else:
                acc = res[len(shifts):]
            for d, dq in zip(shifts, res):
                dqs[d] = dq if d == 0 else shift(dq, 0, -d)
        dq_rows += [dqs[d] for d in range(SIDE)]
        parts = lax.all_to_all(prev, "seq", 0, 0, tiled=True)
        parts = parts.reshape(SIDE, SIDE, 2, TOK, DIM).astype(f32)
        kv_grads.append(jnp.sum(parts, axis=1))

    total = lax.psum(jnp.sum(after(lengths, prev)), "dp")
    mean_len = total.astype(f32) / (2 * lax.axis_size("dp"))
    query_grad = pl.pallas_call(
        place_kernel,
        in_specs=[smem_spec()] * 2 + [vmem_spec()] * (2 * SIDE),
        out_specs=vmem_spec(),
        out_shape=jax.ShapeDtypeStruct(five, bf16),
        compiler_params=params(),
    )(place, mean_len.reshape(1), *dq_rows).reshape(2, TOK, SIDE * GROUP, DIM)
    kv_grad = jnp.transpose(jnp.stack(kv_grads, axis=0) * mean_len, (2, 0, 3, 1, 4)).astype(bf16)
    return (query_grad, kv_grad[0], kv_grad[1])


def solution(mesh):
    spec = P("dp", "seq", None, None)
    return jax.shard_map(
        body,
        mesh=mesh,
        in_specs=(spec,) * 5 + (P("dp"), P("dp")),
        out_specs=(spec,) * 3,
        check_vma=False,
    )
```

```python
import functools
import math

import jax
import jax.numpy as jnp
from jax import lax
from jax.experimental import pallas as pl
from jax.experimental.pallas import tpu as pltpu
from jax.sharding import PartitionSpec as P

f32, bf16 = jnp.float32, jnp.bfloat16
NT = (((1,), (1,)), ((), ()))
NN = (((1,), (0,)), ((), ()))

SIDE = 4
TOK = 128
GROUP = 8
DIM = 128
ROWS = TOK * GROUP
EXTRA = 16
FULL = TOK * SIDE * SIDE
CHUNK = 512
SCALE = 1.0 / math.sqrt(DIM)
EXP2 = SCALE * math.log2(math.e)
VMEM_BYTES = 56 * 1024 * 1024


def shift_pairs(kind, by):
    pairs = []
    for z in range(SIDE):
        for x in range(SIDE):
            to = ((z + by) % SIDE) * SIDE + x if kind == 0 else z * SIDE + (x + by) % SIDE
            pairs.append((z * SIDE + x, to))
    return pairs


def shift(value, kind, by):
    return lax.ppermute(value, "seq", shift_pairs(kind, by % SIDE))


def any_spec():
    return pl.BlockSpec(memory_space=pl.ANY)


def vmem_spec():
    return pl.BlockSpec(memory_space=pltpu.VMEM)


def smem_spec():
    return pl.BlockSpec(memory_space=pltpu.SMEM)


def params():
    return pltpu.CompilerParams(vmem_limit_bytes=VMEM_BYTES)


def pack_kernel(place, q_ref, g_ref, o_ref, *outs):
    for d in range(SIDE):
        head = lax.rem(place[0] + d, SIDE)
        out = outs[d]
        g = g_ref[:, head].reshape(ROWS, DIM)
        o = o_ref[:, head].reshape(ROWS, DIM)
        out[0:ROWS, :] = q_ref[:, head].reshape(ROWS, DIM)
        out[ROWS:2 * ROWS, :] = g
        prod = g.astype(f32) * o.astype(f32)
        high = prod.astype(bf16)
        low = (prod - high.astype(f32)).astype(bf16)
        ones = jnp.ones((8, DIM), bf16)
        delta = lax.dot_general(ones, high, NT, preferred_element_type=f32)
        delta += lax.dot_general(ones, low, NT, preferred_element_type=f32)
        rows = jnp.concatenate(
            [delta[0:1, a * DIM:(a + 1) * DIM] for a in range(ROWS // DIM)], axis=0
        )
        d_high = rows.astype(bf16)
        d_low = (rows - d_high.astype(f32)).astype(bf16)
        out[2 * ROWS:, :] = jnp.concatenate([d_high, d_low], axis=0)


def pack(place, s, query, out_grad, output):
    block = (None, TOK, SIDE, GROUP, DIM)
    spec = pl.BlockSpec(block, lambda i: (s, 0, 0, 0, 0))
    return pl.pallas_call(
        pack_kernel,
        grid=(1,),
        in_specs=[smem_spec()] + [spec] * 3,
        out_specs=[vmem_spec()] * SIDE,
        out_shape=[jax.ShapeDtypeStruct((2 * ROWS + EXTRA, DIM), bf16)] * SIDE,
        compiler_params=params(),
    )(place, query, out_grad, output)


def token_block(z, x, d, e):
    return lax.rem(z - d + SIDE, SIDE) * SIDE + lax.rem(x - e + SIDE, SIDE)


def attention_kernel(seq, shifts, first_call, last_call, *refs):
    count = len(shifts)
    refs = list(refs)
    meta, coef = refs[:2]
    packs = refs[2:2 + count]
    kvs = refs[2 + count:2 + count + SIDE]
    refs = refs[2 + count + SIDE:]
    if not first_call:
        acc_in, refs = refs[:2], refs[2:]
    dqs, refs = refs[:count], refs[count:]
    if last_call:
        dkv, refs = refs[0], refs[1:]
        dka, dva = refs[:2]
        refs = refs[2:]
    else:
        dka, dva = refs[:2]
        refs = refs[2:]
    pk, k_s, v_s, kt_s, p_s, m_s, gm_s, dqt_s, stat, dq_s, sem_p, sem_kv, sem_o = refs
    z, x, length = meta[0], meta[1], meta[2 + seq]
    copies = []
    for e in range(SIDE):
        for d in range(SIDE):
            at, slot = token_block(z, x, d, e), e * SIDE + d
            copies.append(pltpu.make_async_copy(kvs[e].at[d, 0], k_s.at[at], sem_kv.at[0, slot]))
            copies.append(pltpu.make_async_copy(kvs[e].at[d, 1], v_s.at[at], sem_kv.at[1, slot]))
    for d in range(count):
        copies.append(pltpu.make_async_copy(packs[d], pk.at[d], sem_p.at[d]))
    for copy in copies:
        copy.start()
    if first_call:
        dka[...] = jnp.zeros_like(dka)
        dva[...] = jnp.zeros_like(dva)
    else:
        dka[...] = acc_in[0][...]
        dva[...] = acc_in[1][...]
    for copy in copies[:2 * SIDE * SIDE]:
        copy.wait()
    kt_s[...] = k_s[...].reshape(FULL, DIM).T
    factor = coef[seq]
    along = [token_block(z, x, d, 0) for d in shifts]

    def one_block(d, _):
        block = along[0]
        for n in range(1, count):
            block = jnp.where(d == n, along[n], block)
        first = block * TOK
        pltpu.make_async_copy(pk.at[d], pk.at[d], sem_p.at[d]).wait()

        @pl.when(first >= length)
        def _():
            dq_s[d] = jnp.zeros((ROWS, DIM), bf16)

        @pl.when(first < length)
        def _():
            token = lax.broadcasted_iota(jnp.int32, (ROWS, DIM), 0) // GROUP + first
            gm_s[...] = jnp.where(token < length, pk[d, ROWS:2 * ROWS, :], jnp.zeros((), bf16))
            lane_token = lax.broadcasted_iota(jnp.int32, (1, ROWS), 1) // GROUP + first
            tail = pk[d, 2 * ROWS:, :].astype(f32)
            tail = tail[0:8] + tail[8:16]
            delta = jnp.concatenate([tail[a:a + 1, :] for a in range(8)], axis=1)
            delta = jnp.where(lane_token < length, delta, 0.0)
            steps = (first + TOK + CHUNK - 1) // CHUNK

            per = CHUNK // TOK
            rest = lax.rem(block, per) + 1

            def halves(width):
                return 2 if width % 2 == 0 else 1

            def scores_step(c, width, carry, masked):
                parts = halves(width)
                size = width // parts

                def scores(j):
                    s = lax.dot_general(
                        k_s[pl.ds(c * per + j * size, size)].reshape(size * TOK, DIM),
                        pk[d, 0:ROWS, :],
                        NT,
                        preferred_element_type=f32,
                    )
                    if masked:
                        key = lax.broadcasted_iota(jnp.int32, (size * TOK, ROWS), 0)
                        key += c * CHUNK + j * size * TOK
                        s = jnp.where(key <= lane_token, s, -jnp.inf)
                    return s

                top, total = carry
                held = scores(0)
                for j in range(parts):
                    later = scores(j + 1) if j + 1 < parts else None
                    new = jnp.maximum(top, jnp.max(held, axis=0, keepdims=True))
                    p = jnp.exp2((held - new) * EXP2)
                    k0 = pl.multiple_of(c * CHUNK + j * size * TOK, TOK)
                    p_s[pl.ds(k0, size * TOK), :] = p
                    m_s[c * 2 + j] = jnp.broadcast_to(new, (8, ROWS))
                    total = total * jnp.exp2((top - new) * EXP2)
                    total += jnp.sum(p, axis=0, keepdims=True)
                    top, held = new, later
                return top, total

            carry = (jnp.full((1, ROWS), -1e30, f32), jnp.zeros((1, ROWS), f32))
            carry = lax.fori_loop(
                0, steps - 1, lambda c, held: scores_step(c, per, held, False), carry
            )
            for width in range(1, per + 1):

                @pl.when(rest == width)
                def _():
                    row_top, row_total = scores_step(steps - 1, width, carry, True)
                    stat[0:1, :] = row_top
                    stat[8:9, :] = row_total

            top, total = stat[0:1, :], stat[8:9, :]
            inverse = 1.0 / total
            dqt_s[...] = jnp.zeros_like(dqt_s)

            def grads_step(c, width):
                parts = halves(width)
                size = width // parts

                def keys_at(j):
                    return pl.ds(pl.multiple_of(c * CHUNK + j * size * TOK, TOK), size * TOK)

                def dprob(j):
                    return lax.dot_general(
                        v_s[pl.ds(c * per + j * size, size)].reshape(size * TOK, DIM),
                        gm_s[...],
                        NT,
                        preferred_element_type=f32,
                    )

                def add(j, low, ds):
                    at = keys_at(j)
                    dva[at, :] += lax.dot_general(low, gm_s[...], NN, preferred_element_type=f32)
                    dka[at, :] += lax.dot_general(
                        ds, pk[d, 0:ROWS, :], NN, preferred_element_type=f32
                    )
                    dqt_s[...] += lax.dot_general(kt_s[:, at], ds, NN, preferred_element_type=f32)

                dp, ready = dprob(0), None
                for j in range(parts):
                    later = dprob(j + 1) if j + 1 < parts else None
                    weight = jnp.exp2((m_s[c * 2 + j][0:1] - top) * EXP2) * inverse
                    prob = p_s[keys_at(j), :] * weight
                    ds = (prob * (dp - delta)).astype(bf16)
                    low = prob.astype(bf16)
                    if ready is not None:
                        add(*ready)
                    ready, dp = (j, low, ds), later
                add(*ready)

            def full_step(c, _):
                grads_step(c, per)
                return 0

            lax.fori_loop(0, steps - 1, full_step, 0)
            for width in range(1, per + 1):

                @pl.when(rest == width)
                def _():
                    grads_step(steps - 1, width)

            dq_s[d] = (dqt_s[...].T * (factor * SCALE)).astype(bf16)

        return 0

    lax.fori_loop(0, count, one_block, 0)
    outs = [pltpu.make_async_copy(dq_s.at[d], dqs[d], sem_o.at[d]) for d in range(count)]
    for copy in outs:
        copy.start()
    if last_call:
        for b in range(FULL // TOK):
            at = pl.ds(b * TOK, TOK)
            dkv[b, 0] = (dka[at, :] * (factor * SCALE)).astype(bf16)
            dkv[b, 1] = (dva[at, :] * factor).astype(bf16)
    for copy in outs:
        copy.wait()


def attention(meta, coef, seq, shifts, packs, kvs, acc_in=None, last_call=True):
    count = len(packs)
    first_call = acc_in is None
    acc = jax.ShapeDtypeStruct((FULL, DIM), f32)
    acc_scratch = [pltpu.VMEM((FULL, DIM), f32)] * 2
    out_shape = [jax.ShapeDtypeStruct((ROWS, DIM), bf16)] * count
    out_specs = [any_spec()] * count
    if last_call:
        out_shape += [jax.ShapeDtypeStruct((FULL // TOK, 2, TOK, DIM), bf16)]
        out_specs += [vmem_spec()]
    else:
        out_shape += [acc, acc]
        out_specs += [vmem_spec()] * 2
    return pl.pallas_call(
        functools.partial(attention_kernel, seq, shifts, first_call, last_call),
        in_specs=[smem_spec(), smem_spec()]
        + [any_spec()] * (count + SIDE)
        + [vmem_spec()] * (0 if first_call else 2),
        out_specs=out_specs,
        out_shape=out_shape,
        scratch_shapes=(acc_scratch if last_call else [])
        + [
            pltpu.VMEM((count, 2 * ROWS + EXTRA, DIM), bf16),
            pltpu.VMEM((FULL // TOK, TOK, DIM), bf16),
            pltpu.VMEM((FULL // TOK, TOK, DIM), bf16),
            pltpu.VMEM((DIM, FULL), bf16),
            pltpu.VMEM((FULL, ROWS), f32),
            pltpu.VMEM((2 * FULL // CHUNK, 8, ROWS), f32),
            pltpu.VMEM((ROWS, DIM), bf16),
            pltpu.VMEM((DIM, ROWS), f32),
            pltpu.VMEM((16, ROWS), f32),
            pltpu.VMEM((count, ROWS, DIM), bf16),
            pltpu.SemaphoreType.DMA((count,)),
            pltpu.SemaphoreType.DMA((2, SIDE * SIDE)),
            pltpu.SemaphoreType.DMA((count,)),
        ],
        compiler_params=params(),
        cost_estimate=pl.CostEstimate(
            flops=2 * ROWS * FULL * DIM * 5 * count,
            bytes_accessed=8 << 20,
            transcendentals=ROWS * FULL * count,
        ),
    )(meta, coef, *packs, *kvs, *(() if first_call else acc_in))


def place_kernel(place, mean_len, *refs):
    rows, out = refs[:-1], refs[-1]
    for s in range(2):
        for d in range(SIDE):
            head = lax.rem(place[0] + d, SIDE)
            grad = rows[s * SIDE + d][...].astype(f32) * mean_len[0]
            out[s, :, head] = grad.astype(bf16).reshape(TOK, GROUP, DIM)


ROUNDS = (((3, 0, 1, 2),), ((2, 1, 3, 0),))


def after(value, other):
    return lax.optimization_barrier((value, other))[0]


def pack_kv_kernel(place, kv_ref, *outs):
    for d in range(SIDE):
        outs[d][...] = kv_ref[lax.rem(place[0] + d, SIDE)]


def body(query, keys, values, output, out_grad, lengths, margins):
    index = lax.axis_index("seq")
    z, x = index // SIDE, index % SIDE
    place = jnp.concatenate([jnp.stack([z, x]).astype(jnp.int32), lengths])
    weight = jax.nn.sigmoid(-margins)
    signs = jnp.array([-1.0, 1.0], f32)
    coef = jnp.repeat(weight, 2) * signs * 4.0 / lengths.astype(f32)

    kv = jnp.stack([keys, values], axis=1)
    kv = jnp.transpose(kv, (3, 0, 1, 2, 4))
    kv_parts = pl.pallas_call(
        pack_kv_kernel,
        in_specs=[smem_spec(), vmem_spec()],
        out_specs=[vmem_spec()] * SIDE,
        out_shape=[jax.ShapeDtypeStruct((2, 2, TOK, DIM), bf16)] * SIDE,
        compiler_params=params(),
    )(place, kv)
    kv_in = [kv_parts[0]] + [shift(kv_parts[d], 0, d) for d in range(1, SIDE)]
    five = (2, TOK, SIDE, GROUP, DIM)
    query, out_grad, output = (a.reshape(five) for a in (query, out_grad, output))
    query = after(query, kv_parts)
    packs = [pack(place, s, query, out_grad, output) for s in range(2)]
    kv_in = after(kv_in, packs[0])
    gathered = []
    for s in range(2):
        mine = jnp.stack([part[s] for part in kv_in], axis=0)
        gathered.append([mine] + [shift(mine, 1, e) for e in (1, 2, 3)])

    moved = []
    for s in range(2):
        mine = packs[s] if s == 0 else after(packs[s], gathered[0])
        moved.append([mine[0]] + [shift(mine[d], 0, d) for d in range(1, SIDE)])

    dq_rows, kv_grads, prev = [], [], None
    for s in range(2):
        meta = place if s == 0 else after(place, prev)
        acc, dqs = None, {}
        for n, shifts in enumerate(ROUNDS[s]):
            last = n == len(ROUNDS[s]) - 1
            packs_now = [moved[s][d] for d in shifts]
            res = attention(meta, coef, s, shifts, packs_now, gathered[s], acc, last)
            if last:
                prev = after(res[len(shifts)], list(dqs.values()) + dq_rows)
            else:
                acc = res[len(shifts):]
            for d, dq in zip(shifts, res):
                dqs[d] = dq if d == 0 else shift(dq, 0, -d)
        dq_rows += [dqs[d] for d in range(SIDE)]
        parts = lax.all_to_all(prev, "seq", 0, 0, tiled=True)
        parts = parts.reshape(SIDE, SIDE, 2, TOK, DIM).astype(f32)
        kv_grads.append(jnp.sum(parts, axis=1))

    total = lax.psum(jnp.sum(after(lengths, prev)), "dp")
    mean_len = total.astype(f32) / (2 * lax.axis_size("dp"))
    query_grad = pl.pallas_call(
        place_kernel,
        in_specs=[smem_spec()] * 2 + [vmem_spec()] * (2 * SIDE),
        out_specs=vmem_spec(),
        out_shape=jax.ShapeDtypeStruct(five, bf16),
        compiler_params=params(),
    )(place, mean_len.reshape(1), *dq_rows).reshape(2, TOK, SIDE * GROUP, DIM)
    kv_grad = jnp.transpose(jnp.stack(kv_grads, axis=0) * mean_len, (2, 0, 3, 1, 4)).astype(bf16)
    return (query_grad, kv_grad[0], kv_grad[1])


def solution(mesh):
    spec = P("dp", "seq", None, None)
    return jax.shard_map(
        body,
        mesh=mesh,
        in_specs=(spec,) * 5 + (P("dp"), P("dp")),
        out_specs=(spec,) * 3,
        check_vma=False,
    )
```
